768 devices in a mesh: wide: 64 (over y, x, core), grp: 12 (over z).
Axes of the slice: x: 4, y: 8, z: 12, core: 2. Of those that a mesh axis runs over, the one named last changes fastest.
Arguments:
- table: bfloat16 [786432, 256], P(('wide', 'grp')), may hold values from -4 to 4
- item_weight: bfloat16 [256, 1024], replicated, may hold values from -1.5 to 1.5
- ids: int32 [393216], P(('wide', 'grp')), may hold values from 0 to 786431, as said below
- queries: bfloat16 [24576, 1024], P(('wide', 'grp')), may hold values from -7 to 7
- memory: bfloat16 [3, 24576, 1024], P(None, ('wide', 'grp')), may hold values from -4 to 4
- slot_age: int32 [3, 24576], P(None, ('wide', 'grp')), may hold values from 0 to 5
- positive: int32 [768, 32], P(('wide', 'grp')), may hold values from 0 to 31, each once within a row
Outputs:
- loss: float32 [24576], P(('wide', 'grp'))
- table_grad: float32 [786432, 256], P(('wide', 'grp'))
The draws below stay inside these ranges and needn't reach their ends.
Inputs may be any that keep to these rules, and one draw needn't show every extreme that they name: The ids of a device name rows of exactly four devices with the device's wide index, exactly 128 ids for each of the four; one of the four is the same for all devices of one wide index. Ids may repeat. `slot_age`: only whether an age is at most 3 matters; ages may travel in any encoding.
All inputs are finite; a program needn't handle non-finite values.
Results may differ from the reference program's by a relative error of at most 0.0007.
The reference program's roundings to bfloat16 on the way (of `looked`, `pooled`, `items`, `coef` and `item_grad`) count: a program that leaves them out, or rounds other values in their place, can miss the bound.
Values may be sent and summed in bfloat16 or wider, within the bound.
A program may use at most 64 MiB of HBM per device.

```python
import math
import jax
import jax.numpy as jnp
from jax import lax

EMB = 256
DIM = 1024
BAG = 16
MEMS = 3
BATCH_DEV = 32
ROWS_DEV = 1024
IDS_DEV = 512
CAP = 128
ITEMS = 24576
ROWS = 786432
N_WIDE = 64
N_GRP = 12
DEVICES = 768


def stale_parts(key):
    first = jax.random.fold_in(key, 0)
    normal_part = jnp.clip(jax.random.normal(first, (MEMS, ITEMS, DIM), jnp.float32), -4.0, 4.0)
    return normal_part


def draw_memory(key, part):
    normal_part = stale_parts(key)
    values = normal_part
    return values.astype(jnp.bfloat16)


def draw_queries(key, part):
    key = jax.random.fold_in(key, 9)
    first = jax.random.fold_in(key, 0)
    base = jnp.clip(jax.random.normal(first, (ITEMS, DIM), jnp.float32), -3.8, 3.8)
    values = base
    return values.astype(jnp.bfloat16)


def draw_ids(key, part):
    key = jax.random.fold_in(key, 11)
    first, second, third, fourth = jax.random.split(key, 4)
    device_ids = jnp.arange(DEVICES, dtype=jnp.int32)
    shared_owner = jax.random.randint(first, (N_WIDE,), 0, N_GRP, dtype=jnp.int32)
    shared_dev = shared_owner[device_ids // N_GRP]
    offsets = jax.vmap(lambda k: jax.random.permutation(k, N_GRP - 1))(jax.random.split(second, DEVICES)).astype(jnp.int32)
    others = (shared_dev[:, None] + 1 + offsets) % N_GRP
    orders = jnp.concatenate([shared_dev[:, None], others], axis=1)
    spots = jnp.arange(IDS_DEV, dtype=jnp.int32)
    rank = spots // CAP
    owner_grp = orders[:, rank]
    shuffles = jax.vmap(lambda k: jax.random.permutation(k, IDS_DEV))(jax.random.split(third, DEVICES)).astype(jnp.int32)
    owner_grp = jnp.take_along_axis(owner_grp, shuffles, axis=1)
    owner = device_ids[:, None] // N_GRP * N_GRP + owner_grp
    local_rows = jax.random.randint(fourth, (DEVICES, IDS_DEV), 0, ROWS_DEV, dtype=jnp.int32)
    return (owner * ROWS_DEV + local_rows).reshape(-1).astype(jnp.int32)


def touch_ends(array, rng, least, top_value):
    longest = array.shape.index(max(array.shape))
    spots = []
    for shift in (0, 1):
        where = [jax.random.randint(jax.random.fold_in(rng, axis), (), 0, length) for axis, length in enumerate(array.shape)]
        where[longest] = (where[longest] + shift) % array.shape[longest]
        spots.append(tuple(where))
    return array.at[spots[0]].set(least).at[spots[1]].set(top_value)


def levels(rng, extent, shards, least, largest):
    factor_of = 1.0
    for axis_at, blocks in shards:
        steps = jax.random.uniform(jax.random.fold_in(jax.random.fold_in(rng, 6), axis_at), (blocks,), jnp.float32, least / len(shards), largest / len(shards))
        factor_of = factor_of * jnp.repeat(jnp.exp(steps), extent[axis_at] // blocks).reshape((-1,) + (1,) * (len(extent) - 1 - axis_at))
    return factor_of


def noise(own_key, extent, spread, most, shards=(), kind=jnp.bfloat16):
    factor_of = levels(own_key, extent, shards, -0.22, 0.18) if shards else 1.0
    array = jax.random.normal(own_key, extent, jnp.float32) * spread * factor_of
    return jnp.minimum(jnp.maximum(array, -most), most).astype(kind)


def setup_inputs(seed: int = 0) -> dict:
    arg_keys = jax.random.split(jax.random.key(seed), 8)
    table = noise(arg_keys[0], (ROWS, EMB), 1.0, 4.0, ((0, 768),))
    item_weight = noise(arg_keys[1], (EMB, DIM), (EMB // 16) ** -0.5, 1.5)
    ids = draw_ids(jax.random.fold_in(arg_keys[7], 71), 0)
    queries = draw_queries(jax.random.fold_in(arg_keys[7], 71), 0)
    memory = draw_memory(jax.random.fold_in(arg_keys[7], 71), 0)
    slot_age = touch_ends(jax.random.randint(arg_keys[5], (MEMS, ITEMS), 0, 2 * MEMS), jax.random.fold_in(arg_keys[5], 1), 0, (2 * MEMS) - 1).astype(jnp.int32)
    positive = jax.vmap(lambda own: jax.random.permutation(own, BATCH_DEV))(jax.random.split(arg_keys[6], DEVICES)).reshape((DEVICES, BATCH_DEV)).astype(jnp.int32)
    return {"table": table, "item_weight": item_weight, "ids": ids, "queries": queries, "memory": memory, "slot_age": slot_age, "positive": positive}


def group_lse(packed):
    query_block, item_block, stale_block, age_block = packed
    factor = 2.0 / math.sqrt(DIM)
    current = jnp.dot(query_block, item_block.T, preferred_element_type=jnp.float32) * factor
    stale_scores = jnp.einsum('qd,snd->qsn', query_block.astype(jnp.float32), stale_block.astype(jnp.float32)) * factor
    alive = (age_block <= MEMS)[None]
    highest = jnp.maximum(lax.optimization_barrier(jnp.max(current, axis=1)), lax.optimization_barrier(jnp.max(jnp.where(alive, stale_scores, -jnp.inf), axis=(1, 2))))
    summed = lax.optimization_barrier(jnp.sum(jnp.exp(current - highest[:, None]), axis=1))
    summed = summed + lax.optimization_barrier(jnp.sum(jnp.where(alive, jnp.exp(stale_scores - highest[:, None, None]), 0.0), axis=(1, 2)))
    return highest + jnp.log(summed)

def reference(table, item_weight, ids, queries, memory, slot_age, positive):
    factor = 2.0 / math.sqrt(DIM)
    looked = table[ids]
    pooled = (lax.optimization_barrier(jnp.sum(looked.astype(jnp.float32).reshape(ITEMS, BAG, EMB), axis=1)) / BAG).astype(jnp.bfloat16)
    items = jnp.dot(pooled, item_weight, preferred_element_type=jnp.float32).astype(jnp.bfloat16)
    width_all = N_WIDE * BATCH_DEV
    items_grouped = items.reshape(N_WIDE, N_GRP, BATCH_DEV, DIM).transpose(1, 0, 2, 3).reshape(N_GRP, width_all, DIM)
    queries_grouped = queries.reshape(N_WIDE, N_GRP, BATCH_DEV, DIM).transpose(1, 0, 2, 3).reshape(N_GRP, width_all, DIM)
    memory_grouped = memory.reshape(MEMS, N_WIDE, N_GRP, BATCH_DEV, DIM).transpose(2, 0, 1, 3, 4).reshape(N_GRP, MEMS, width_all, DIM)
    ages_grouped = slot_age.reshape(MEMS, N_WIDE, N_GRP, BATCH_DEV).transpose(2, 0, 1, 3).reshape(N_GRP, MEMS, width_all)
    lse = lax.map(group_lse, (queries_grouped, items_grouped, memory_grouped, ages_grouped))
    lse = lse.reshape(N_GRP, N_WIDE, BATCH_DEV).transpose(1, 0, 2).reshape(DEVICES, BATCH_DEV)
    query_dev = queries.reshape(DEVICES, BATCH_DEV, DIM).astype(jnp.float32)
    item_dev = items.reshape(DEVICES, BATCH_DEV, DIM).astype(jnp.float32)
    own = jnp.einsum('dqe,dke->dqk', query_dev, item_dev) * factor
    chosen = positive[:, :, None] == jnp.arange(BATCH_DEV, dtype=jnp.int32)[None, None, :]
    loss = (lse - lax.optimization_barrier(jnp.sum(jnp.where(chosen, own, 0.0), axis=2))).reshape(ITEMS)
    coef = (jnp.exp(own - lse[:, :, None]) - chosen.astype(jnp.float32)).astype(jnp.bfloat16)
    item_grad = (jnp.einsum('dqk,dqe->dke', coef.astype(jnp.float32), query_dev) * factor).astype(jnp.bfloat16)
    item_grad = item_grad.reshape(ITEMS, DIM)
    pooled_grad = jnp.dot(item_grad, item_weight.T, preferred_element_type=jnp.float32)
    id_grad = jnp.repeat(pooled_grad, BAG, axis=0) / BAG
    table_grad = jnp.zeros((ROWS, EMB), jnp.float32).at[ids].add(id_grad)
    return (loss, table_grad)
```

```python
import math

import jax
import jax.numpy as jnp
from jax import lax
from jax.experimental import pallas as pl
from jax.experimental.pallas import tpu as pltpu
from jax.sharding import PartitionSpec as P

MESH = pl.DeviceIdType.MESH
NX, NY, NC, NZ = 4, 8, 2, 12
NQ = NY * NC
DEAD = -1e30
NT = (((1,), (1,)), ((), ()))
NN = (((1,), (0,)), ((), ()))
f32, bf16, i32 = jnp.float32, jnp.bfloat16, jnp.int32


def wrap(a, n):
    return jnp.where(a >= n, a - n, a)


def kernel(
    table, weight, meta, queries, memory,
    loss, grad,
    meta_z, meta_x, mem_x, yq, zq, psend, precv, pool_x, part, parts, coef_all,
    count, q4, items, pg_hi, pg_lo,
    ms, mr, xs, xr, es, er, ys, yr, cs, cr, zs, zr, ps, pr, os, orr, ls, lr, gs, gr,
):
    wide = lax.axis_index("wide")
    z = lax.axis_index("grp")
    y, x, c = wide // (NX * NC), (wide // NC) % NX, wide % NC
    q = c * NY + y
    factor = 2.0 / math.sqrt(queries.shape[1])
    base = (wide * NZ + z) * table.shape[0]
    rows = table.shape[0]
    nb = queries.shape[0]

    def dev(y_, x_, c_, z_):
        return ((y_ * NX + x_) * NC + c_, z_)

    def zdev(k):
        return dev(y, x, c, wrap(z + k, NZ))

    def xdev(k):
        return dev(y, (x + k) % NX, c, z)

    def ydev(k):
        return dev((y + k) % NY, x, c, z)

    def qdev(k):
        qq = (q + k) % NQ
        return dev(qq % NY, x, qq // NY, z)

    def rc(src, dst, s, r, to):
        return pltpu.make_async_remote_copy(src, dst, s, r, device_id=to, device_id_type=MESH)

    def loop(lo, hi, body):
        lax.fori_loop(lo, hi, lambda k, t: (body(k), t)[1], 0)

    barrier = pltpu.get_barrier_semaphore()

    def greet(to):
        pl.semaphore_signal(barrier, inc=1, device_id=to, device_id_type=MESH)

    loop(1, NZ, lambda k: greet(zdev(k)))
    loop(1, NQ, lambda k: greet(qdev(k)))
    loop(1, NX, lambda k: greet(xdev(k)))

    meta_z[z] = meta[...]
    meta_x[x] = meta[...]
    zq[z] = queries[...]
    yq[c, y] = queries[...]
    mem_x[x] = memory[...]
    for j in range(4):
        q4[j] = queries[...]
    pl.semaphore_wait(barrier, (NZ - 1) + (NQ - 1) + (NX - 1))

    def c_meta_z(k):
        return rc(meta, meta_z.at[z], ms.at[k], mr.at[k], zdev(k))

    def c_meta_x(k):
        return rc(meta, meta_x.at[x], xs.at[k], xr.at[k], xdev(k))

    def c_mem_x(k):
        return rc(memory, mem_x.at[x], es.at[k], er.at[k], xdev(k))

    def c_q_y(k):
        return rc(queries, yq.at[c, y], ys.at[k], yr.at[k], ydev(k))

    def c_q_c():
        return rc(yq.at[c], yq.at[c], cs, cr, dev(y, x, 1 - c, z))

    def c_ring(d, s):
        owner = wrap(z + s, NZ) if d == 0 else wrap(z - s + NZ, NZ)
        to = zdev(NZ - 1) if d == 0 else zdev(1)
        return rc(zq.at[owner], zq.at[owner], zs.at[d, s], zr.at[d, s], to)

    def ring_start(s):
        if s > 0:
            c_ring(0, s - 1).wait_recv()
            c_ring(1, s - 1).wait_recv()
        c_ring(0, s).start()
        if s < NZ // 2 - 1:
            c_ring(1, s).start()

    def c_part(k):
        return rc(psend.at[k], precv.at[z], ps.at[k], pr.at[k], zdev(k))

    def c_pool(k):
        return rc(pool_x.at[x], pool_x.at[x], os.at[k], orr.at[k], xdev(k))

    def c_lse(k):
        return rc(part.at[((q + k) % NQ) // 4], parts.at[q], ls.at[k], lr.at[k], qdev(k))

    def c_coef(k):
        return rc(coef_all.at[z], coef_all.at[z], gs.at[k], gr.at[k], zdev(k))

    loop(1, NZ, lambda k: c_meta_z(k).start())
    ring_start(0)
    loop(1, NX, lambda k: c_meta_x(k).start())
    loop(1, NX, lambda k: c_mem_x(k).start())
    loop(1, NY, lambda k: c_q_y(k).start())

    def partial_sums(owner):
        cols = jnp.transpose(meta_z[owner] - base)
        spots = lax.broadcasted_iota(i32, (nb, rows), 1)
        found = jnp.zeros((nb, rows), f32)
        for r in range(4):
            for b in range(4):
                col = cols[b * nb : (b + 1) * nb, r : r + 1]
                found = found + jnp.where(col == spots, 1.0, 0.0)
        return lax.dot_general(found.astype(bf16), table[...], NN, preferred_element_type=f32)

    loop(1, NZ, lambda k: c_meta_z(k).wait_recv())
    ring_start(1)

    def lookup(j):
        k = 6 + (1 - 2 * (j % 2)) * ((j + 1) // 2)
        psend[k] = partial_sums(wrap(z + k, NZ))
        c_part(k).start()

    loop(0, 4, lookup)
    ring_start(2)
    loop(4, NZ - 1, lookup)
    precv[z] = partial_sums(z)
    ring_start(3)

    loop(1, NY, lambda k: c_q_y(k).wait_recv())
    c_q_c().start()

    lane = lax.broadcasted_iota(i32, (8, 128), 1) // nb

    def counts(g):
        ids = []
        for b in range(4):
            lined = jnp.zeros((8, 128), i32)
            for d in range(4):
                rolled = meta_z[4 * g + d] - base
                if d != b:
                    rolled = pltpu.roll(rolled, ((d - b) * nb) % 128, 1)
                lined = jnp.where(lane == d, rolled, lined)
            ids.append(lined)
        step = 128

        def block(t):
            spots = lax.broadcasted_iota(i32, (step, 128), 0) + t * step
            found = jnp.zeros((step, 128), f32)
            for b in range(4):
                for r in range(4):
                    found = found + jnp.where(ids[b][r : r + 1, :] == spots, 1.0, 0.0)
            count[g, pl.ds(pl.multiple_of(t * step, step), step), :] = found.astype(bf16)

        loop(0, rows // step, block)

    for g in range(3):
        counts(g)
    ring_start(4)

    loop(1, NX, lambda k: c_meta_x(k).wait_recv())
    loop(1, NX, lambda k: c_mem_x(k).wait_recv())
    c_q_c().wait_recv()
    all_q = yq[...].reshape(NQ * nb, queries.shape[1])

    high = jnp.full((1, NQ * nb), DEAD, f32)
    total = jnp.zeros((1, NQ * nb), f32)

    def stale(t, carry):
        high, total = carry
        keys = mem_x[t].reshape(3 * nb, queries.shape[1])
        score = lax.dot_general(keys, all_q, NT, preferred_element_type=f32) * factor
        ages = jnp.transpose(meta_x[t])
        age = jnp.concatenate([ages[0:nb, 5 + s : 6 + s] for s in range(3)], axis=0)
        score = jnp.where(age <= 3, score, DEAD)
        new = jnp.maximum(high, jnp.max(score, axis=0, keepdims=True))
        total = total * jnp.exp(high - new) + jnp.sum(jnp.exp(score - new), axis=0, keepdims=True)
        return new, total

    high, total = lax.fori_loop(0, NX, stale, (high, total))

    loop(1, NZ, lambda k: c_part(k).wait_recv())
    pooled = precv[0]
    for s in range(1, NZ):
        pooled = pooled + precv[s]
    pool_x[x] = (pooled / 16.0).astype(bf16)
    loop(1, NX, lambda k: c_pool(k).start())
    ring_start(5)
    loop(1, NX, lambda k: c_pool(k).wait_recv())
    every = pool_x[...].reshape(NX * nb, table.shape[1])
    items[...] = lax.dot_general(every, weight[...], NN, preferred_element_type=f32).astype(bf16)

    score = lax.dot_general(items[...], all_q, NT, preferred_element_type=f32) * factor
    new = jnp.maximum(high, jnp.max(score, axis=0, keepdims=True))
    total = total * jnp.exp(high - new) + jnp.sum(jnp.exp(score - new), axis=0, keepdims=True)
    for g in range(4):
        part[g, 0:1, :] = new[:, 128 * g : 128 * (g + 1)]
        part[g, 1:2, :] = total[:, 128 * g : 128 * (g + 1)]
    parts[q] = part[q // 4]
    loop(1, NQ, lambda k: c_lse(k).start())

    mine = items[pl.ds(pl.multiple_of(x * nb, nb), nb), :]
    own = lax.dot_general(
        mine, q4[...].reshape(4 * nb, queries.shape[1]), NT, preferred_element_type=f32
    ) * factor
    chosen = meta[4:5, :] == lax.broadcasted_iota(i32, (nb, 128), 0)
    hit = jnp.sum(jnp.where(chosen, own, 0.0), axis=0, keepdims=True)
    lanes = lax.broadcasted_iota(i32, (nb, 128), 1) // nb

    loop(1, NQ, lambda k: c_lse(k).wait_recv())
    got = parts[...]
    highs, totals = got[:, 0, :], got[:, 1, :]
    top = jnp.max(highs, axis=0, keepdims=True)
    lse = top + jnp.log(jnp.sum(totals * jnp.exp(highs - top), axis=0, keepdims=True))
    lse = jnp.where(lanes[0:1] == q % 4, lse, 0.0)
    lse = lse + pltpu.roll(lse, 64, 1)
    lse = lse + pltpu.roll(lse, 32, 1)
    loss[...] = lse - hit
    coef = jnp.exp(own - lse) - jnp.where(chosen, 1.0, 0.0)
    coef_all[z] = jnp.where(lanes == z % 4, coef, 0.0).astype(bf16)
    loop(1, NZ, lambda k: c_coef(k).start())

    c_ring(0, NZ // 2 - 1).wait_recv()
    loop(1, NZ, lambda k: c_coef(k).wait_recv())
    for g in range(3):
        held = coef_all[4 * g : 4 * g + 4].reshape(4 * nb, 128)
        asked = zq[4 * g : 4 * g + 4].reshape(4 * nb, queries.shape[1])
        item_grad = (
            lax.dot_general(held, asked, NN, preferred_element_type=f32) * factor
        ).astype(bf16)
        pooled_grad = lax.dot_general(item_grad, weight[...], NT, preferred_element_type=f32) / 16.0
        upper = pooled_grad.astype(bf16)
        pg_hi[g] = upper
        pg_lo[g] = (pooled_grad - upper.astype(f32)).astype(bf16)

    def spread(t):
        step = 256
        spot = pl.ds(pl.multiple_of(t * step, step), step)
        out = jnp.zeros((step, table.shape[1]), f32)
        for g in range(3):
            found = count[g, spot, :]
            out = out + lax.dot_general(found, pg_hi[g], NN, preferred_element_type=f32)
            out = out + lax.dot_general(found, pg_lo[g], NN, preferred_element_type=f32)
        grad[spot, :] = out

    loop(0, rows // 256, spread)

    loop(1, NZ, lambda k: c_meta_z(k).wait_send())
    loop(1, NX, lambda k: c_meta_x(k).wait_send())
    loop(1, NX, lambda k: c_mem_x(k).wait_send())
    loop(1, NY, lambda k: c_q_y(k).wait_send())
    c_q_c().wait_send()
    for s in range(NZ // 2):
        c_ring(0, s).wait_send()
        if s < NZ // 2 - 1:
            c_ring(1, s).wait_send()
    loop(1, NZ, lambda k: c_part(k).wait_send())
    loop(1, NX, lambda k: c_pool(k).wait_send())
    loop(1, NQ, lambda k: c_lse(k).wait_send())
    loop(1, NZ, lambda k: c_coef(k).wait_send())


def body(table, item_weight, ids, queries, memory, slot_age, positive):
    nb, dim = queries.shape
    rows, emb = table.shape
    meta = jnp.concatenate(
        [
            ids.reshape(nb, 16).T.reshape(4, 4 * nb),
            jnp.tile(positive, (1, 4)),
            jnp.tile(slot_age, (1, 4)),
        ],
        axis=0,
    )
    vmem = pl.BlockSpec(memory_space=pltpu.VMEM)
    dma = pltpu.SemaphoreType.DMA
    loss, grad = pl.pallas_call(
        kernel,
        out_shape=(
            jax.ShapeDtypeStruct((1, 128), f32),
            jax.ShapeDtypeStruct((rows, emb), f32),
        ),
        in_specs=[vmem] * 5,
        out_specs=(vmem, vmem),
        scratch_shapes=[
            pltpu.VMEM((NZ, 8, 128), i32),
            pltpu.VMEM((NX, 8, 128), i32),
            pltpu.VMEM((NX, 3, nb, dim), bf16),
            pltpu.VMEM((NC, NY, nb, dim), bf16),
            pltpu.VMEM((NZ, nb, dim), bf16),
            pltpu.VMEM((NZ, nb, emb), f32),
            pltpu.VMEM((NZ, nb, emb), f32),
            pltpu.VMEM((NX, nb, emb), bf16),
            pltpu.VMEM((4, 8, 128), f32),
            pltpu.VMEM((NQ, 8, 128), f32),
            pltpu.VMEM((NZ, nb, 128), bf16),
            pltpu.VMEM((3, rows, 128), bf16),
            pltpu.VMEM((4, nb, dim), bf16),
            pltpu.VMEM((NX * nb, dim), bf16),
            pltpu.VMEM((3, 128, emb), bf16),
            pltpu.VMEM((3, 128, emb), bf16),
            dma((NZ,)), dma((NZ,)),
            dma((NX,)), dma((NX,)),
            dma((NX,)), dma((NX,)),
            dma((NY,)), dma((NY,)),
            dma, dma,
            dma((2, NZ // 2)), dma((2, NZ // 2)),
            dma((NZ,)), dma((NZ,)),
            dma((NX,)), dma((NX,)),
            dma((NQ,)), dma((NQ,)),
            dma((NZ,)), dma((NZ,)),
        ],
        compiler_params=pltpu.CompilerParams(
            collective_id=0, has_side_effects=True, vmem_limit_bytes=40 * 1024 * 1024
        ),
        name="step",
    )(table, item_weight, meta, queries, memory)
    return loss[0, :nb], grad


def solution(mesh):
    split = P(("wide", "grp"))
    rows = P(("wide", "grp"), None)
    return jax.shard_map(
        body,
        mesh=mesh,
        in_specs=(
            rows, P(), split, rows, P(None, ("wide", "grp"), None), P(None, ("wide", "grp")), rows,
        ),
        out_specs=(split, rows),
        check_vma=False,
    )
```

```python
import math

import jax
import jax.numpy as jnp
from jax import lax
from jax.experimental import pallas as pl
from jax.experimental.pallas import tpu as pltpu
from jax.sharding import PartitionSpec as P

MESH = pl.DeviceIdType.MESH
NX, NY, NC, NZ = 4, 8, 2, 12
NQ = NY * NC
DEAD = -1e30
NT = (((1,), (1,)), ((), ()))
NN = (((1,), (0,)), ((), ()))
f32, bf16, i32 = jnp.float32, jnp.bfloat16, jnp.int32


def wrap(a, n):
    return jnp.where(a >= n, a - n, a)


class Copies:
    def __init__(self, make, ks):
        self.make, self.ks = make, ks

    def each(self, act):
        if isinstance(self.ks, range):
            lax.fori_loop(self.ks[0], self.ks[-1] + 1, lambda k, t: (act(self.make(k)), t)[1], 0)
        else:
            for k in self.ks:
                act(self.make(k))

    def only(self, *ks):
        return Copies(self.make, ks)

    def start(self):
        self.each(lambda copy: copy.start())

    def recv(self):
        self.each(lambda copy: copy.wait_recv())

    def sent(self):
        self.each(lambda copy: copy.wait_send())


def kernel(
    table_hbm, weight_hbm, ids_hbm, queries_hbm, memory_hbm, ages_hbm, positive_hbm,
    loss, grad,
    table, weight, ids, label, ages, meta, marks, cols,
    meta_z, meta_x, mem_x, yq, zq, psend, precv, relayed, pool_x, part, parts, coef_all,
    count, q4, items, pg_hi, pg_lo,
    ds, ms, mr, xs, xr, es, er, hs, hr, ys, yr, cs, cr, zs, zr, ps, pr, rs, rr, os, orr, ls, lr, gs, gr,
):
    wide = lax.axis_index("wide")
    z = lax.axis_index("grp")
    y, x, c = wide // (NX * NC), (wide // NC) % NX, wide % NC
    q = c * NY + y
    nb, dim = queries_hbm.shape
    factor = 2.0 / math.sqrt(dim)
    rows, emb = table_hbm.shape
    base = (wide * NZ + z) * rows

    def dev(y_, x_, c_, z_):
        return ((y_ * NX + x_) * NC + c_, z_)

    def zdev(k):
        return dev(y, x, c, wrap(z + k, NZ))

    def xdev(k):
        return dev(y, (x + k) % NX, c, z)

    def ydev(k):
        return dev((y + k) % NY, x, c, z)

    def qdev(k):
        qq = (q + k) % NQ
        return dev(qq % NY, x, qq // NY, z)

    def rc(src, dst, s, r, to):
        return pltpu.make_async_remote_copy(src, dst, s, r, device_id=to, device_id_type=MESH)

    def loop(lo, hi, body):
        lax.fori_loop(lo, hi, lambda k, t: (body(k), t)[1], 0)

    opened = []

    def start(*kinds):
        for kind in kinds:
            kind.start()
            opened.append(kind)

    def recv(*kinds):
        for kind in kinds:
            kind.recv()

    loads = [
        pltpu.make_async_copy(src, dst, ds.at[n])
        for n, (src, dst) in enumerate(
            [(ids_hbm, ids.at[0:4]), (positive_hbm, label), (ages_hbm, ages), (memory_hbm, mem_x.at[x])]
            + [(queries_hbm, dst) for dst in [yq.at[c, y], zq.at[z]] + [q4.at[j] for j in range(4)]]
            + [(table_hbm, table), (weight_hbm, weight)]
        )
    ]
    for load in loads:
        load.start()

    barrier = pltpu.get_barrier_semaphore()

    def greet(to):
        pl.semaphore_signal(barrier, inc=1, device_id=to, device_id_type=MESH)

    loop(1, NZ, lambda k: greet(zdev(k)))
    loop(1, NQ, lambda k: greet(qdev(k)))
    loop(1, NX, lambda k: greet(xdev(k)))

    ids[4:8] = jnp.zeros((4, 128), i32)
    marks[...] = jnp.zeros((8, 128), i32)
    for load in loads[:3]:
        load.wait()
    cols[...] = jnp.transpose(ids[...])
    marks[4:5, 0:nb] = label[...]
    marks[5:8, 0:nb] = ages[...]
    spot = lax.broadcasted_iota(i32, (8, 8), 1)
    byte = [cols[pl.ds(b, 8, stride=16), :] for b in range(16)]
    lines = []
    for b in range(4):
        for r in range(4):
            line = jnp.zeros((8, 8), i32)
            for t in range(4):
                line = jnp.where(spot == t, byte[4 * t + b][:, r : r + 1], line)
            lines.append(line)
    lined = jnp.transpose(jnp.concatenate(lines, axis=0))
    marked = marks[...]
    marked = marked + pltpu.roll(marked, 32, 1)
    marked = marked + pltpu.roll(marked, 64, 1)
    own_meta = jnp.where(lax.broadcasted_iota(i32, (8, 128), 0) < 4, lined, marked)
    meta[...] = own_meta
    meta_z[z] = own_meta
    meta_x[x] = own_meta
    for load in loads[3:10]:
        load.wait()
    pl.semaphore_wait(barrier, (NZ - 1) + (NQ - 1) + (NX - 1))

    def ring(s, d):
        owner = wrap(z + s, NZ) if d == 0 else wrap(z - s + NZ, NZ)
        to = zdev(NZ - 1) if d == 0 else zdev(1)
        return rc(zq.at[owner], zq.at[owner], zs.at[d, s], zr.at[d, s], to)

    def half(r):
        block = mem_x.at[(x + 1 + 2 * r) % NX, :, nb // 2 * r : nb // 2 * (r + 1)]
        return rc(block, block, hs.at[r], hr.at[r], xdev(3 - 2 * r))

    def fourth(_):
        block = yq.at[c, (y + 3) % NY]
        return rc(block, block, ys.at[4], yr.at[4], ydev(NY - 1))

    def across(k):
        block = yq.at[c, (y - k + NY) % NY]
        return rc(block, block, cs.at[k], cr.at[k], dev(y, x, 1 - c, z))

    def relay(j):
        to = zdev(jnp.where(j == 2, NZ - 1, 2 - j))
        return rc(psend.at[far(j)], relayed.at[j], rs.at[j], rr.at[j], to)

    def far(j):
        return 6 + (1 - 2 * (j % 2)) * ((j + 1) // 2)

    def near(j):
        d = 3 - j // 2
        return jnp.where(j % 2 == 0, d, NZ - d)

    c_meta_z = Copies(lambda k: rc(meta, meta_z.at[z], ms.at[k], mr.at[k], zdev(k)), range(1, NZ))
    c_meta_x = Copies(lambda k: rc(meta, meta_x.at[x], xs.at[k], xr.at[k], xdev(k)), range(1, NX))
    c_mem_x = Copies(lambda k: rc(mem_x.at[x], mem_x.at[x], es.at[k], er.at[k], xdev(k)), (1, 3))
    c_half = Copies(half, (0, 1))
    c_q_y = Copies(
        lambda k: rc(yq.at[c, y], yq.at[c, y], ys.at[k], yr.at[k], ydev(k)), (5, 3, 6, 2, 7, 1)
    )
    c_fourth = Copies(fourth, (4,))
    c_across = Copies(across, range(0, NY))
    c_ring = [
        Copies(lambda d, s=s: ring(s, d), (0, 1) if s < NZ // 2 - 1 else (0,)) for s in range(NZ // 2)
    ]
    c_relay = Copies(relay, range(0, 3))
    c_part = Copies(
        lambda k: rc(psend.at[k], precv.at[k], ps.at[k], pr.at[k], zdev(k)), (1, 11, 2, 10, 3, 9, 4, 8)
    )
    c_pool = Copies(
        lambda k: rc(pool_x.at[x], pool_x.at[x], os.at[k], orr.at[k], xdev(k)), (2, 1, 3)
    )
    c_lse = Copies(
        lambda k: rc(part.at[((q + k) % NQ) // 4], parts.at[q], ls.at[k], lr.at[k], qdev(k)),
        range(1, NQ),
    )
    c_coef = Copies(
        lambda k: rc(coef_all.at[z], coef_all.at[z], gs.at[k], gr.at[k], zdev(k)), range(1, NZ)
    )

    def ring_start(s):
        if s > 0:
            recv(c_ring[s - 1])
        start(c_ring[s])

    start(c_meta_z, c_meta_x, c_mem_x, c_q_y, c_across.only(0))

    def partial_sums(owner):
        wanted = jnp.transpose(meta_z[owner] - base)
        spots = lax.broadcasted_iota(i32, (nb, rows), 1)
        found = jnp.zeros((nb, rows), f32)
        for r in range(4):
            for b in range(4):
                col = wanted[b * nb : (b + 1) * nb, r : r + 1]
                found = found + jnp.where(col == spots, 1.0, 0.0)
        return lax.dot_general(found.astype(bf16), table[...], NN, preferred_element_type=f32)

    recv(c_meta_z.only(3, 9, 2, 10, 1, 11))
    ring_start(0)
    for load in loads[10:]:
        load.wait()

    def lookup_near(j):
        k = near(j)
        psend[k] = partial_sums(wrap(z + k, NZ))
        c_part.make(k).start()

    def lookup_far(j):
        k = far(j)
        psend[k] = partial_sums(wrap(z + k, NZ))
        relay(j).start()

    def lookup_fourth(j):
        k = far(j)
        psend[k] = partial_sums(wrap(z + k, NZ))

    loop(0, 6, lookup_near)
    recv(c_meta_z.only(6, 5, 7, 4, 8))
    loop(0, 3, lookup_far)
    recv(c_mem_x)
    start(c_half)
    loop(3, 5, lookup_fourth)
    precv[0] = partial_sums(z)
    recv(c_relay)
    psend[4] = psend[4] + (relayed[0] + relayed[1])
    psend[8] = psend[8] + relayed[2]
    start(c_part.only(4, 8))
    opened.extend([c_part.only(1, 11, 2, 10, 3, 9), c_relay])
    ring_start(1)

    recv(c_q_y.only(5))
    start(c_fourth)
    for k in (7, 1, 6, 2, 5, 3):
        if k != 5:
            recv(c_q_y.only(k))
        start(c_across.only(k))

    recv(c_part)
    pooled = precv[0]
    for k in (1, 11, 2, 10, 3, 9, 4, 8):
        pooled = pooled + precv[k]
    pool_x[x] = (pooled / 16.0).astype(bf16)
    start(c_pool)
    recv(c_fourth)
    start(c_across.only(4))
    ring_start(2)

    recv(c_meta_x, c_half, c_across)
    all_q = yq[...].reshape(NQ * nb, dim)

    high = jnp.full((1, NQ * nb), DEAD, f32)
    total = jnp.zeros((1, NQ * nb), f32)

    def stale(t, carry):
        high, total = carry
        keys = mem_x[t].reshape(3 * nb, dim)
        score = lax.dot_general(keys, all_q, NT, preferred_element_type=f32) * factor
        marked = jnp.transpose(meta_x[t])
        age = jnp.concatenate([marked[0:nb, 5 + s : 6 + s] for s in range(3)], axis=0)
        score = jnp.where(age <= 3, score, DEAD)
        new = jnp.maximum(high, jnp.max(score, axis=0, keepdims=True))
        total = total * jnp.exp(high - new) + jnp.sum(jnp.exp(score - new), axis=0, keepdims=True)
        return new, total

    high, total = lax.fori_loop(0, NX, stale, (high, total))

    recv(c_pool)
    every = pool_x[...].reshape(NX * nb, emb)
    items[...] = lax.dot_general(every, weight[...], NN, preferred_element_type=f32).astype(bf16)

    score = lax.dot_general(items[...], all_q, NT, preferred_element_type=f32) * factor
    new = jnp.maximum(high, jnp.max(score, axis=0, keepdims=True))
    total = total * jnp.exp(high - new) + jnp.sum(jnp.exp(score - new), axis=0, keepdims=True)
    for g in range(4):
        part[g, 0:1, :] = new[:, 128 * g : 128 * (g + 1)]
        part[g, 1:2, :] = total[:, 128 * g : 128 * (g + 1)]
    parts[q] = part[q // 4]
    start(c_lse)
    ring_start(3)

    mine = items[pl.ds(pl.multiple_of(x * nb, nb), nb), :]
    own = lax.dot_general(
        mine, q4[...].reshape(4 * nb, dim), NT, preferred_element_type=f32
    ) * factor
    chosen = meta[4:5, :] == lax.broadcasted_iota(i32, (nb, 128), 0)
    hit = jnp.sum(jnp.where(chosen, own, 0.0), axis=0, keepdims=True)
    lanes = lax.broadcasted_iota(i32, (nb, 128), 1) // nb

    lane = lax.broadcasted_iota(i32, (8, 128), 1) // nb

    def counts(g):
        ids = []
        for b in range(4):
            lined = jnp.zeros((8, 128), i32)
            for d in range(4):
                rolled = meta_z[4 * g + d] - base
                if d != b:
                    rolled = pltpu.roll(rolled, ((d - b) * nb) % 128, 1)
                lined = jnp.where(lane == d, rolled, lined)
            ids.append(lined)
        step = 128

        def block(t):
            spots = lax.broadcasted_iota(i32, (step, 128), 0) + t * step
            found = jnp.zeros((step, 128), f32)
            for b in range(4):
                for r in range(4):
                    found = found + jnp.where(ids[b][r : r + 1, :] == spots, 1.0, 0.0)
            count[g, pl.ds(pl.multiple_of(t * step, step), step), :] = found.astype(bf16)

        loop(0, rows // step, block)

    counts(0)
    ring_start(4)
    recv(c_lse)
    got = parts[...]
    highs, totals = got[:, 0, :], got[:, 1, :]
    top = jnp.max(highs, axis=0, keepdims=True)
    lse = top + jnp.log(jnp.sum(totals * jnp.exp(highs - top), axis=0, keepdims=True))
    lse = jnp.where(lanes[0:1] == q % 4, lse, 0.0)
    lse = lse + pltpu.roll(lse, 64, 1)
    lse = lse + pltpu.roll(lse, 32, 1)
    loss[...] = lse - hit
    coef = jnp.exp(own - lse) - jnp.where(chosen, 1.0, 0.0)
    coef_all[z] = jnp.where(lanes == z % 4, coef, 0.0).astype(bf16)
    start(c_coef)
    ring_start(5)
    counts(1)
    counts(2)

    recv(c_ring[NZ // 2 - 1], c_coef)
    for g in range(3):
        held = coef_all[4 * g : 4 * g + 4].reshape(4 * nb, 128)
        asked = zq[4 * g : 4 * g + 4].reshape(4 * nb, dim)
        item_grad = (
            lax.dot_general(held, asked, NN, preferred_element_type=f32) * factor
        ).astype(bf16)
        pooled_grad = lax.dot_general(item_grad, weight[...], NT, preferred_element_type=f32) / 16.0
        upper = pooled_grad.astype(bf16)
        pg_hi[g] = upper
        pg_lo[g] = (pooled_grad - upper.astype(f32)).astype(bf16)

    def spread(t):
        step = 256
        spot = pl.ds(pl.multiple_of(t * step, step), step)
        out = jnp.zeros((step, emb), f32)
        for g in range(3):
            found = count[g, spot, :]
            out = out + lax.dot_general(found, pg_hi[g], NN, preferred_element_type=f32)
            out = out + lax.dot_general(found, pg_lo[g], NN, preferred_element_type=f32)
        grad[spot, :] = out

    loop(0, rows // 256, spread)

    for kind in opened:
        kind.sent()


def body(table, item_weight, ids, queries, memory, slot_age, positive):
    nb, dim = queries.shape
    rows, emb = table.shape
    arguments = (table, item_weight, ids.reshape(4, 4 * nb), queries, memory, slot_age, positive)
    vmem = pl.BlockSpec(memory_space=pltpu.VMEM)
    dma = pltpu.SemaphoreType.DMA
    loss, grad = pl.pallas_call(
        kernel,
        out_shape=(
            jax.ShapeDtypeStruct((1, 128), f32),
            jax.ShapeDtypeStruct((rows, emb), f32),
        ),
        in_specs=[pl.BlockSpec(memory_space=pltpu.HBM)] * 7,
        out_specs=(vmem, vmem),
        scratch_shapes=[
            pltpu.VMEM((rows, emb), bf16),
            pltpu.VMEM((emb, dim), bf16),
            pltpu.VMEM((8, 128), i32),
            pltpu.VMEM((1, nb), i32),
            pltpu.VMEM((3, nb), i32),
            pltpu.VMEM((8, 128), i32),
            pltpu.VMEM((8, 128), i32),
            pltpu.VMEM((128, 8), i32),
            pltpu.VMEM((NZ, 8, 128), i32),
            pltpu.VMEM((NX, 8, 128), i32),
            pltpu.VMEM((NX, 3, nb, dim), bf16),
            pltpu.VMEM((NC, NY, nb, dim), bf16),
            pltpu.VMEM((NZ, nb, dim), bf16),
            pltpu.VMEM((NZ, nb, emb), f32),
            pltpu.VMEM((NZ, nb, emb), f32),
            pltpu.VMEM((3, nb, emb), f32),
            pltpu.VMEM((NX, nb, emb), bf16),
            pltpu.VMEM((4, 8, 128), f32),
            pltpu.VMEM((NQ, 8, 128), f32),
            pltpu.VMEM((NZ, nb, 128), bf16),
            pltpu.VMEM((3, rows, 128), bf16),
            pltpu.VMEM((4, nb, dim), bf16),
            pltpu.VMEM((NX * nb, dim), bf16),
            pltpu.VMEM((3, 128, emb), bf16),
            pltpu.VMEM((3, 128, emb), bf16),
            dma((12,)),
            dma((NZ,)), dma((NZ,)),
            dma((NX,)), dma((NX,)),
            dma((NX,)), dma((NX,)),
            dma((2,)), dma((2,)),
            dma((NY,)), dma((NY,)),
            dma((NY,)), dma((NY,)),
            dma((2, NZ // 2)), dma((2, NZ // 2)),
            dma((NZ,)), dma((NZ,)),
            dma((3,)), dma((3,)),
            dma((NX,)), dma((NX,)),
            dma((NQ,)), dma((NQ,)),
            dma((NZ,)), dma((NZ,)),
        ],
        compiler_params=pltpu.CompilerParams(
            collective_id=0, has_side_effects=True, vmem_limit_bytes=40 * 1024 * 1024
        ),
        name="step",
    )(*(pltpu.with_memory_space_constraint(a, pltpu.HBM) for a in arguments))
    return loss[0, :nb], grad


def solution(mesh):
    split = P(("wide", "grp"))
    rows = P(("wide", "grp"), None)
    return jax.shard_map(
        body,
        mesh=mesh,
        in_specs=(
            rows, P(), split, rows, P(None, ("wide", "grp"), None), P(None, ("wide", "grp")), rows,
        ),
        out_specs=(split, rows),
        check_vma=False,
    )
```

```python
import math

import jax
import jax.numpy as jnp
from jax import lax
from jax.experimental import pallas as pl
from jax.experimental.pallas import tpu as pltpu
from jax.sharding import PartitionSpec as P

MESH = pl.DeviceIdType.MESH
NX, NY, NC, NZ = 4, 8, 2, 12
NQ = NY * NC
DEAD = -1e30
FAR_Z = (6, 5, 7, 4, 8, 3, 9, 2, 10, 1, 11)
FAR_Q = (4, 12, 3, 5, 11, 13, 2, 6, 10, 14, 1, 7, 9, 15, 8)
FAR_X = (2, 1, 3)
NT = (((1,), (1,)), ((), ()))
NN = (((1,), (0,)), ((), ()))
TN = (((0,), (0,)), ((), ()))
f32, bf16, i32 = jnp.float32, jnp.bfloat16, jnp.int32


def wrap(a, n):
    return jnp.where(a >= n, a - n, a)


class Copies:
    def __init__(self, make, ks):
        self.make, self.ks = make, ks

    def each(self, act):
        if isinstance(self.ks, range):
            lax.fori_loop(self.ks[0], self.ks[-1] + 1, lambda k, t: (act(self.make(k)), t)[1], 0)
        else:
            for k in self.ks:
                act(self.make(k))

    def only(self, *ks):
        return Copies(self.make, ks)

    def start(self):
        self.each(lambda copy: copy.start())

    def recv(self):
        self.each(lambda copy: copy.wait_recv())

    def sent(self):
        self.each(lambda copy: copy.wait_send())


def kernel(
    table_hbm, weight_hbm, ids_hbm, queries_hbm, memory_hbm, ages_hbm, positive_hbm,
    loss, grad,
    table, weight, ids, label, ages, meta, marks, cols,
    meta_z, meta_x, mem_x, yq, zq, psend, precv, relayed, pool_x, part, parts, coef_all,
    count, q4, items, parted,
    ds, ms, mr, xs, xr, es, er, hs, hr, ys, yr, cs, cr, zs, zr, ps, pr, rs, rr, os, orr, ls, lr, gs, gr,
):
    wide = lax.axis_index("wide")
    z = lax.axis_index("grp")
    y, x, c = wide // (NX * NC), (wide // NC) % NX, wide % NC
    q = c * NY + y
    nb, dim = queries_hbm.shape
    factor = 2.0 / math.sqrt(dim)
    rows, emb = table_hbm.shape
    base = (wide * NZ + z) * rows

    def dev(y_, x_, c_, z_):
        return ((y_ * NX + x_) * NC + c_, z_)

    def zdev(k):
        return dev(y, x, c, wrap(z + k, NZ))

    def xdev(k):
        return dev(y, (x + k) % NX, c, z)

    def ydev(k):
        return dev((y + k) % NY, x, c, z)

    def qdev(k):
        qq = (q + k) % NQ
        return dev(qq % NY, x, qq // NY, z)

    def rc(src, dst, s, r, to):
        return pltpu.make_async_remote_copy(src, dst, s, r, device_id=to, device_id_type=MESH)

    def loop(lo, hi, body):
        lax.fori_loop(lo, hi, lambda k, t: (body(k), t)[1], 0)

    opened = []

    def start(*kinds):
        for kind in kinds:
            kind.start()
            opened.append(kind)

    def recv(*kinds):
        for kind in kinds:
            kind.recv()

    loads = [
        pltpu.make_async_copy(src, dst, ds.at[n])
        for n, (src, dst) in enumerate(
            [(ids_hbm, ids.at[0:4]), (positive_hbm, label), (ages_hbm, ages), (memory_hbm, mem_x.at[x])]
            + [(queries_hbm, dst) for dst in [yq.at[c, y], zq.at[z]] + [q4.at[j] for j in range(4)]]
            + [(table_hbm, table), (weight_hbm, weight)]
        )
    ]
    for load in loads:
        load.start()

    barrier = pltpu.get_barrier_semaphore()

    def greet(to):
        pl.semaphore_signal(barrier, inc=1, device_id=to, device_id_type=MESH)

    for k in FAR_Z:
        greet(zdev(k))
    for k in FAR_Q:
        greet(qdev(k))
    for k in FAR_X:
        greet(xdev(k))

    ids[4:8] = jnp.zeros((4, 128), i32)
    marks[...] = jnp.zeros((8, 128), i32)
    for load in loads[:3]:
        load.wait()
    cols[...] = jnp.transpose(ids[...])
    marks[4:5, 0:nb] = label[...]
    marks[5:8, 0:nb] = ages[...]
    spot = lax.broadcasted_iota(i32, (8, 8), 1)
    byte = [cols[pl.ds(b, 8, stride=16), :] for b in range(16)]
    lines = []
    for b in range(4):
        for r in range(4):
            line = jnp.zeros((8, 8), i32)
            for t in range(4):
                line = jnp.where(spot == t, byte[4 * t + b][:, r : r + 1], line)
            lines.append(line)
    lined = jnp.transpose(jnp.concatenate(lines, axis=0))
    marked = marks[...]
    marked = marked + pltpu.roll(marked, 32, 1)
    marked = marked + pltpu.roll(marked, 64, 1)
    own_meta = jnp.where(lax.broadcasted_iota(i32, (8, 128), 0) < 4, lined, marked)
    meta[...] = own_meta
    meta_z[z] = own_meta
    meta_x[x] = own_meta
    for load in loads[3:10]:
        load.wait()
    pl.semaphore_wait(barrier, (NZ - 1) + (NQ - 1) + (NX - 1))

    def ring(s, d):
        owner = wrap(z + s, NZ) if d == 0 else wrap(z - s + NZ, NZ)
        to = zdev(NZ - 1) if d == 0 else zdev(1)
        return rc(zq.at[owner], zq.at[owner], zs.at[d, s], zr.at[d, s], to)

    def half(r):
        block = mem_x.at[(x + 1 + 2 * r) % NX, :, nb // 2 * r : nb // 2 * (r + 1)]
        return rc(block, block, hs.at[r], hr.at[r], xdev(3 - 2 * r))

    def fourth(_):
        block = yq.at[c, (y + 3) % NY]
        return rc(block, block, ys.at[4], yr.at[4], ydev(NY - 1))

    def across(k):
        block = yq.at[c, (y - k + NY) % NY]
        return rc(block, block, cs.at[k], cr.at[k], dev(y, x, 1 - c, z))

    def relay(j):
        to = zdev(jnp.where(j == 2, NZ - 1, 2 - j))
        return rc(psend.at[far(j)], relayed.at[j], rs.at[j], rr.at[j], to)

    def far(j):
        return 6 + (1 - 2 * (j % 2)) * ((j + 1) // 2)

    def apart(g, r):
        u = (r + 1 - z + NZ) % 4
        if g == 0:
            return jnp.where(u == 0, NZ - 1, u - 1)
        return jnp.where(u < 2, u + 3, u + 7) if g == 1 else jnp.where(u < 2, u + 7, u + 3)

    c_meta_z = Copies(lambda k: rc(meta, meta_z.at[z], ms.at[k], mr.at[k], zdev(k)), FAR_Z)
    c_meta_x = Copies(lambda k: rc(meta, meta_x.at[x], xs.at[k], xr.at[k], xdev(k)), range(1, NX))
    c_mem_x = Copies(lambda k: rc(mem_x.at[x], mem_x.at[x], es.at[k], er.at[k], xdev(k)), (1, 3))
    c_half = Copies(half, (0, 1))
    c_q_y = Copies(
        lambda k: rc(yq.at[c, y], yq.at[c, y], ys.at[k], yr.at[k], ydev(k)), (5, 3, 6, 2, 7, 1)
    )
    c_fourth = Copies(fourth, (4,))
    c_across = Copies(across, range(0, NY))
    c_ring = [
        Copies(lambda d, s=s: ring(s, d), (0, 1) if s < NZ // 2 - 1 else (0,)) for s in range(NZ // 2)
    ]
    c_relay = Copies(relay, range(0, 3))
    c_part = Copies(
        lambda k: rc(psend.at[k], precv.at[k], ps.at[k], pr.at[k], zdev(k)), (1, 11, 2, 10, 3, 9, 4, 8)
    )
    c_pool = Copies(
        lambda k: rc(pool_x.at[x], pool_x.at[x], os.at[k], orr.at[k], xdev(k)), FAR_X
    )
    c_lse = Copies(
        lambda k: rc(part.at[((q + k) % NQ) // 4], parts.at[q], ls.at[k], lr.at[k], qdev(k)),
        FAR_Q,
    )
    c_coef = Copies(
        lambda k: rc(coef_all.at[z], coef_all.at[z], gs.at[k], gr.at[k], zdev(k)), FAR_Z
    )

    def ring_start(s):
        if s > 0:
            recv(c_ring[s - 1])
        start(c_ring[s])

    start(c_meta_z, c_q_y.only(5, 3))

    lane = lax.broadcasted_iota(i32, (8, 128), 1) // nb

    def counts(g):
        lined = [jnp.zeros((8, 128), i32) for b in range(4)]
        for r in range(4):
            asked = meta_z[wrap(z + apart(g, r), NZ)] - base
            for b in range(4):
                rolled = asked if r == b else pltpu.roll(asked, ((r - b) * nb) % 128, 1)
                lined[b] = jnp.where(lane == r, rolled, lined[b])
        step = 128

        def block(t):
            spots = lax.broadcasted_iota(i32, (step, 128), 0) + t * step
            found = jnp.zeros((step, 128), f32)
            for b in range(4):
                for r in range(4):
                    found = found + jnp.where(lined[b][r : r + 1, :] == spots, 1.0, 0.0)
            found = found.astype(bf16)
            spot = pl.ds(pl.multiple_of(t * step, step), step)
            count[g, spot, 0:128] = found
            count[g, spot, 128:256] = found

        loop(0, rows // step, block)

    def lookup(g):
        counts(g)
        sums = lax.dot_general(count[g, :, 0:128], table[...], TN, preferred_element_type=f32)
        for r in range(4):
            psend[apart(g, r)] = sums[r * nb : (r + 1) * nb]

    recv(c_meta_z.only(1, 11, 10))
    start(c_meta_x, c_mem_x, c_q_y.only(6, 2, 7, 1), c_across.only(0))
    for load in loads[10:]:
        load.wait()
    lookup(0)
    start(c_part.only(1, 11, 2))
    recv(c_meta_z.only(2, 9, 3, 8))
    ring_start(0)
    lookup(1)
    recv(c_meta_z.only(4, 7, 5, 6))
    lookup(2)
    start(c_relay)
    start(c_part.only(10, 3, 9))
    recv(c_q_y.only(5))
    start(c_fourth)
    recv(c_relay)
    psend[4] = psend[4] + (relayed[0] + relayed[1])
    psend[8] = psend[8] + relayed[2]
    start(c_part.only(4, 8))
    ring_start(1)

    recv(c_mem_x)
    start(c_half)
    for k in (7, 1, 6, 2, 5, 3):
        if k != 5:
            recv(c_q_y.only(k))
        start(c_across.only(k))

    recv(c_part)
    pooled = psend[0]
    for k in (1, 11, 2, 10, 3, 9, 4, 8):
        pooled = pooled + precv[k]
    pool_x[x] = (pooled / 16.0).astype(bf16)
    start(c_pool)
    recv(c_fourth)
    start(c_across.only(4))
    ring_start(2)

    recv(c_meta_x, c_half, c_across)
    all_q = yq[...].reshape(NQ * nb, dim)

    high = jnp.full((1, NQ * nb), DEAD, f32)
    total = jnp.zeros((1, NQ * nb), f32)

    def stale(t, carry):
        high, total = carry
        keys = mem_x[t].reshape(3 * nb, dim)
        score = lax.dot_general(keys, all_q, NT, preferred_element_type=f32) * factor
        marked = jnp.transpose(meta_x[t])
        age = jnp.concatenate([marked[0:nb, 5 + s : 6 + s] for s in range(3)], axis=0)
        score = jnp.where(age <= 3, score, DEAD)
        new = jnp.maximum(high, jnp.max(score, axis=0, keepdims=True))
        total = total * jnp.exp(high - new) + jnp.sum(jnp.exp(score - new), axis=0, keepdims=True)
        return new, total

    high, total = lax.fori_loop(0, NX, stale, (high, total))

    recv(c_pool)
    every = pool_x[...].reshape(NX * nb, emb)
    items[...] = lax.dot_general(every, weight[...], NN, preferred_element_type=f32).astype(bf16)

    score = lax.dot_general(items[...], all_q, NT, preferred_element_type=f32) * factor
    new = jnp.maximum(high, jnp.max(score, axis=0, keepdims=True))
    total = total * jnp.exp(high - new) + jnp.sum(jnp.exp(score - new), axis=0, keepdims=True)
    for g in range(4):
        part[g, 0:1, :] = new[:, 128 * g : 128 * (g + 1)]
        part[g, 1:2, :] = total[:, 128 * g : 128 * (g + 1)]
    parts[q] = part[q // 4]
    start(c_lse)
    ring_start(3)

    mine = items[pl.ds(pl.multiple_of(x * nb, nb), nb), :]
    own = lax.dot_general(
        mine, q4[...].reshape(4 * nb, dim), NT, preferred_element_type=f32
    ) * factor
    chosen = meta[4:5, :] == lax.broadcasted_iota(i32, (nb, 128), 0)
    hit = jnp.sum(jnp.where(chosen, own, 0.0), axis=0, keepdims=True)
    lanes = lax.broadcasted_iota(i32, (nb, 128), 1) // nb

    ring_start(4)
    recv(c_lse)
    got = parts[...]
    highs, totals = got[:, 0, :], got[:, 1, :]
    top = jnp.max(highs, axis=0, keepdims=True)
    lse = top + jnp.log(jnp.sum(totals * jnp.exp(highs - top), axis=0, keepdims=True))
    lse = jnp.where(lanes[0:1] == q % 4, lse, 0.0)
    lse = lse + pltpu.roll(lse, 64, 1)
    lse = lse + pltpu.roll(lse, 32, 1)
    loss[...] = lse - hit
    coef = jnp.exp(own - lse) - jnp.where(chosen, 1.0, 0.0)
    coef_all[z] = jnp.where(lanes == z % 4, coef, 0.0).astype(bf16)
    start(c_coef)
    ring_start(5)

    def gradient(g):
        who = [wrap(z + apart(g, r), NZ) for r in range(4)]
        held = jnp.concatenate([coef_all[w] for w in who], axis=0)
        asked = jnp.concatenate([zq[w] for w in who], axis=0)
        item_grad = (
            lax.dot_general(held, asked, NN, preferred_element_type=f32) * factor
        ).astype(bf16)
        pooled_grad = lax.dot_general(item_grad, weight[...], NT, preferred_element_type=f32) / 16.0
        upper = pooled_grad.astype(bf16)
        parted[0:128, :] = upper
        parted[128:256, :] = (pooled_grad - upper.astype(f32)).astype(bf16)

        def spread(t):
            step = 256
            spot = pl.ds(pl.multiple_of(t * step, step), step)
            added = lax.dot_general(count[g, spot, :], parted[...], NN, preferred_element_type=f32)
            grad[spot, :] = added if g == 0 else grad[spot, :] + added

        loop(0, rows // 256, spread)

    for kind in opened:
        if kind is not c_coef and kind is not c_ring[NZ // 2 - 1]:
            kind.sent()
    recv(c_coef.only(1, 11, 10))
    gradient(0)
    recv(c_coef.only(2, 9, 3, 8))
    gradient(1)
    c_coef.sent()
    c_ring[NZ // 2 - 1].sent()
    recv(c_ring[NZ // 2 - 1], c_coef.only(4, 7, 5, 6))
    gradient(2)


def body(table, item_weight, ids, queries, memory, slot_age, positive):
    nb, dim = queries.shape
    rows, emb = table.shape
    arguments = (table, item_weight, ids.reshape(4, 4 * nb), queries, memory, slot_age, positive)
    vmem = pl.BlockSpec(memory_space=pltpu.VMEM)
    dma = pltpu.SemaphoreType.DMA
    loss, grad = pl.pallas_call(
        kernel,
        out_shape=(
            jax.ShapeDtypeStruct((1, 128), f32),
            jax.ShapeDtypeStruct((rows, emb), f32),
        ),
        in_specs=[pl.BlockSpec(memory_space=pltpu.HBM)] * 7,
        out_specs=(vmem, vmem),
        scratch_shapes=[
            pltpu.VMEM((rows, emb), bf16),
            pltpu.VMEM((emb, dim), bf16),
            pltpu.VMEM((8, 128), i32),
            pltpu.VMEM((1, nb), i32),
            pltpu.VMEM((3, nb), i32),
            pltpu.VMEM((8, 128), i32),
            pltpu.VMEM((8, 128), i32),
            pltpu.VMEM((128, 8), i32),
            pltpu.VMEM((NZ, 8, 128), i32),
            pltpu.VMEM((NX, 8, 128), i32),
            pltpu.VMEM((NX, 3, nb, dim), bf16),
            pltpu.VMEM((NC, NY, nb, dim), bf16),
            pltpu.VMEM((NZ, nb, dim), bf16),
            pltpu.VMEM((NZ, nb, emb), f32),
            pltpu.VMEM((NZ, nb, emb), f32),
            pltpu.VMEM((3, nb, emb), f32),
            pltpu.VMEM((NX, nb, emb), bf16),
            pltpu.VMEM((4, 8, 128), f32),
            pltpu.VMEM((NQ, 8, 128), f32),
            pltpu.VMEM((NZ, nb, 128), bf16),
            pltpu.VMEM((3, rows, 256), bf16),
            pltpu.VMEM((4, nb, dim), bf16),
            pltpu.VMEM((NX * nb, dim), bf16),
            pltpu.VMEM((256, emb), bf16),
            dma((12,)),
            dma((NZ,)), dma((NZ,)),
            dma((NX,)), dma((NX,)),
            dma((NX,)), dma((NX,)),
            dma((2,)), dma((2,)),
            dma((NY,)), dma((NY,)),
            dma((NY,)), dma((NY,)),
            dma((2, NZ // 2)), dma((2, NZ // 2)),
            dma((NZ,)), dma((NZ,)),
            dma((3,)), dma((3,)),
            dma((NX,)), dma((NX,)),
            dma((NQ,)), dma((NQ,)),
            dma((NZ,)), dma((NZ,)),
        ],
        compiler_params=pltpu.CompilerParams(
            collective_id=0, has_side_effects=True, vmem_limit_bytes=40 * 1024 * 1024
        ),
        name="step",
    )(*(pltpu.with_memory_space_constraint(a, pltpu.HBM) for a in arguments))
    return loss[0, :nb], grad


def solution(mesh):
    split = P(("wide", "grp"))
    rows = P(("wide", "grp"), None)
    return jax.shard_map(
        body,
        mesh=mesh,
        in_specs=(
            rows, P(), split, rows, P(None, ("wide", "grp"), None), P(None, ("wide", "grp")), rows,
        ),
        out_specs=(split, rows),
        check_vma=False,
    )
```

```python
import math

import jax
import jax.numpy as jnp
from jax import lax
from jax.experimental import pallas as pl
from jax.experimental.pallas import tpu as pltpu
from jax.sharding import PartitionSpec as P

MESH = pl.DeviceIdType.MESH
NX, NY, NC, NZ = 4, 8, 2, 12
NQ = NY * NC
DEAD = -1e30
FAR_Z = (6, 5, 7, 4, 8, 3, 9, 2, 10, 1, 11)
FAR_Q = (4, 12, 3, 5, 11, 13, 2, 6, 10, 14, 1, 7, 9, 15, 8)
FAR_X = (2, 1, 3)
NT = (((1,), (1,)), ((), ()))
NN = (((1,), (0,)), ((), ()))
TN = (((0,), (0,)), ((), ()))
f32, bf16, i32 = jnp.float32, jnp.bfloat16, jnp.int32


def wrap(a, n):
    return jnp.where(a >= n, a - n, a)


class Copies:
    def __init__(self, make, ks):
        self.make, self.ks = make, ks

    def each(self, act):
        if isinstance(self.ks, range):
            lax.fori_loop(self.ks[0], self.ks[-1] + 1, lambda k, t: (act(self.make(k)), t)[1], 0)
        else:
            for k in self.ks:
                act(self.make(k))

    def only(self, *ks):
        return Copies(self.make, ks)

    def start(self):
        self.each(lambda copy: copy.start())

    def recv(self):
        self.each(lambda copy: copy.wait_recv())

    def sent(self):
        self.each(lambda copy: copy.wait_send())


def kernel(
    table_hbm, weight_hbm, ids_hbm, queries_hbm, memory_hbm, ages_hbm, positive_hbm,
    loss, grad,
    table, weight, ids, label, ages, meta, marks, cols,
    meta_z, meta_x, mem_x, yq, zq, psend, precv, relayed, pool_x, part, parts, coef_all,
    count, q4, items, parted,
    ds, ms, mr, xs, xr, es, er, hs, hr, ys, yr, cs, cr, zs, zr, ps, pr, rs, rr, os, orr, ls, lr, gs, gr,
):
    wide = lax.axis_index("wide")
    z = lax.axis_index("grp")
    y, x, c = wide // (NX * NC), (wide // NC) % NX, wide % NC
    q = c * NY + y
    nb, dim = queries_hbm.shape
    factor = 2.0 / math.sqrt(dim)
    rows, emb = table_hbm.shape
    base = (wide * NZ + z) * rows

    def dev(y_, x_, c_, z_):
        return ((y_ * NX + x_) * NC + c_, z_)

    def zdev(k):
        return dev(y, x, c, wrap(z + k, NZ))

    def xdev(k):
        return dev(y, (x + k) % NX, c, z)

    def ydev(k):
        return dev((y + k) % NY, x, c, z)

    def qdev(k):
        qq = (q + k) % NQ
        return dev(qq % NY, x, qq // NY, z)

    def rc(src, dst, s, r, to):
        return pltpu.make_async_remote_copy(src, dst, s, r, device_id=to, device_id_type=MESH)

    def loop(lo, hi, body):
        lax.fori_loop(lo, hi, lambda k, t: (body(k), t)[1], 0)

    opened = []

    def start(*kinds):
        for kind in kinds:
            kind.start()
            opened.append(kind)

    def recv(*kinds):
        for kind in kinds:
            kind.recv()

    loads = [
        pltpu.make_async_copy(src, dst, ds.at[n])
        for n, (src, dst) in enumerate(
            [(ids_hbm, ids.at[0:4]), (positive_hbm, label), (ages_hbm, ages), (memory_hbm, mem_x.at[x])]
            + [(queries_hbm, dst) for dst in [yq.at[c, y], zq.at[z]] + [q4.at[j] for j in range(4)]]
            + [(table_hbm, table), (weight_hbm, weight)]
        )
    ]
    for load in loads:
        load.start()

    barrier = pltpu.get_barrier_semaphore()

    def greet(to):
        pl.semaphore_signal(barrier, inc=1, device_id=to, device_id_type=MESH)

    for k in FAR_Z:
        greet(zdev(k))
    for k in FAR_Q:
        greet(qdev(k))
    for k in FAR_X:
        greet(xdev(k))

    ids[4:8] = jnp.zeros((4, 128), i32)
    marks[...] = jnp.zeros((8, 128), i32)
    for load in loads[:3]:
        load.wait()
    cols[...] = jnp.transpose(ids[...])
    marks[4:5, 0:nb] = label[...]
    marks[5:8, 0:nb] = ages[...]
    spot = lax.broadcasted_iota(i32, (8, 8), 1)
    byte = [cols[pl.ds(b, 8, stride=16), :] for b in range(16)]
    lines = []
    for b in range(4):
        for r in range(4):
            line = jnp.zeros((8, 8), i32)
            for t in range(4):
                line = jnp.where(spot == t, byte[4 * t + b][:, r : r + 1], line)
            lines.append(line)
    lined = jnp.transpose(jnp.concatenate(lines, axis=0))
    marked = marks[...]
    marked = marked + pltpu.roll(marked, 32, 1)
    marked = marked + pltpu.roll(marked, 64, 1)
    own_meta = jnp.where(lax.broadcasted_iota(i32, (8, 128), 0) < 4, lined, marked)
    meta[...] = own_meta
    meta_z[z] = own_meta
    meta_x[x] = own_meta
    for load in loads[3:10]:
        load.wait()
    pl.semaphore_wait(barrier, (NZ - 1) + (NQ - 1) + (NX - 1))

    def ring(s, d):
        owner = wrap(z + s, NZ) if d == 0 else wrap(z - s + NZ, NZ)
        to = zdev(NZ - 1) if d == 0 else zdev(1)
        return rc(zq.at[owner], zq.at[owner], zs.at[d, s], zr.at[d, s], to)

    def half(r):
        block = mem_x.at[(x + 1 + 2 * r) % NX, :, nb // 2 * r : nb // 2 * (r + 1)]
        return rc(block, block, hs.at[r], hr.at[r], xdev(3 - 2 * r))

    def fourth(_):
        block = yq.at[c, (y + 3) % NY]
        return rc(block, block, ys.at[4], yr.at[4], ydev(NY - 1))

    def across(k):
        block = yq.at[c, (y - k + NY) % NY]
        return rc(block, block, cs.at[k], cr.at[k], dev(y, x, 1 - c, z))

    def relay(j):
        to = zdev(jnp.where(j == 2, NZ - 1, 2 - j))
        return rc(psend.at[far(j)], relayed.at[j], rs.at[j], rr.at[j], to)

    def far(j):
        return 6 + (1 - 2 * (j % 2)) * ((j + 1) // 2)

    def apart(g, r):
        u = (r + 1 - z + NZ) % 4
        if g == 0:
            return jnp.where(u == 0, NZ - 1, u - 1)
        return jnp.where(u < 2, u + 3, u + 7) if g == 1 else jnp.where(u < 2, u + 7, u + 3)

    c_meta_z = Copies(lambda k: rc(meta, meta_z.at[z], ms.at[k], mr.at[k], zdev(k)), FAR_Z)
    c_meta_x = Copies(lambda k: rc(meta, meta_x.at[x], xs.at[k], xr.at[k], xdev(k)), range(1, NX))
    c_mem_x = Copies(lambda k: rc(mem_x.at[x], mem_x.at[x], es.at[k], er.at[k], xdev(k)), (1, 3))
    c_half = Copies(half, (0, 1))
    c_q_y = Copies(
        lambda k: rc(yq.at[c, y], yq.at[c, y], ys.at[k], yr.at[k], ydev(k)), (5, 3, 6, 2, 7, 1)
    )
    c_fourth = Copies(fourth, (4,))
    c_across = Copies(across, range(0, NY))
    c_ring = [
        Copies(lambda d, s=s: ring(s, d), (0, 1) if s < NZ // 2 - 1 else (0,)) for s in range(NZ // 2)
    ]
    c_relay = Copies(relay, range(0, 3))
    c_part = Copies(
        lambda k: rc(psend.at[k], precv.at[k], ps.at[k], pr.at[k], zdev(k)), (1, 11, 2, 10, 3, 9, 4, 8)
    )
    c_pool = Copies(
        lambda k: rc(pool_x.at[x], pool_x.at[x], os.at[k], orr.at[k], xdev(k)), FAR_X
    )
    c_lse = Copies(
        lambda k: rc(part.at[((q + k) % NQ) // 4], parts.at[q], ls.at[k], lr.at[k], qdev(k)),
        FAR_Q,
    )
    c_coef = Copies(
        lambda k: rc(coef_all.at[z], coef_all.at[z], gs.at[k], gr.at[k], zdev(k)), FAR_Z
    )

    def ring_start(s):
        if s > 0:
            recv(c_ring[s - 1])
        start(c_ring[s])

    start(c_meta_z, c_q_y.only(5, 3))

    lane = lax.broadcasted_iota(i32, (8, 128), 1) // nb

    def counts(g):
        lined = [jnp.zeros((8, 128), i32) for b in range(4)]
        for r in range(4):
            asked = meta_z[wrap(z + apart(g, r), NZ)] - base
            for b in range(4):
                rolled = asked if r == b else pltpu.roll(asked, ((r - b) * nb) % 128, 1)
                lined[b] = jnp.where(lane == r, rolled, lined[b])
        step = 128

        def block(t):
            spots = lax.broadcasted_iota(i32, (step, 128), 0) + t * step
            found = jnp.zeros((step, 128), f32)
            for b in range(4):
                for r in range(4):
                    found = found + jnp.where(lined[b][r : r + 1, :] == spots, 1.0, 0.0)
            found = found.astype(bf16)
            spot = pl.ds(pl.multiple_of(t * step, step), step)
            count[g, spot, 0:128] = found
            count[g, spot, 128:256] = found

        loop(0, rows // step, block)

    def lookup(g):
        counts(g)
        sums = lax.dot_general(count[g, :, 0:128], table[...], TN, preferred_element_type=f32)
        for r in range(4):
            psend[apart(g, r)] = sums[r * nb : (r + 1) * nb]

    recv(c_meta_z.only(1, 11, 10))
    start(c_meta_x, c_mem_x, c_q_y.only(6, 2, 7, 1), c_across.only(0))
    for load in loads[10:]:
        load.wait()
    lookup(0)
    start(c_part.only(1, 11, 2))
    recv(c_meta_z.only(2, 9, 3, 8))
    ring_start(0)
    lookup(1)
    recv(c_meta_z.only(4, 7, 5, 6))
    lookup(2)
    start(c_relay)
    start(c_part.only(10, 3, 9))
    recv(c_q_y.only(5))
    start(c_fourth)
    recv(c_relay.only(2))
    psend[8] = psend[8] + relayed[2]
    start(c_part.only(8))
    recv(c_relay.only(1, 0))
    psend[4] = psend[4] + (relayed[0] + relayed[1])
    start(c_part.only(4))
    ring_start(1)

    recv(c_mem_x)
    start(c_half)
    for k in (7, 1, 6, 2, 5, 3):
        if k != 5:
            recv(c_q_y.only(k))
        start(c_across.only(k))

    recv(c_part)
    pooled = psend[0]
    for k in (1, 11, 2, 10, 3, 9, 4, 8):
        pooled = pooled + precv[k]
    pool_x[x] = (pooled / 16.0).astype(bf16)
    start(c_pool)
    recv(c_fourth)
    start(c_across.only(4))
    ring_start(2)

    recv(c_meta_x, c_half, c_across)
    all_q = yq[...].reshape(NQ * nb, dim)

    high = jnp.full((1, NQ * nb), DEAD, f32)
    total = jnp.zeros((1, NQ * nb), f32)

    def stale(t, carry):
        high, total = carry
        keys = mem_x[t].reshape(3 * nb, dim)
        score = lax.dot_general(keys, all_q, NT, preferred_element_type=f32) * factor
        marked = jnp.transpose(meta_x[t])
        age = jnp.concatenate([marked[0:nb, 5 + s : 6 + s] for s in range(3)], axis=0)
        score = jnp.where(age <= 3, score, DEAD)
        new = jnp.maximum(high, jnp.max(score, axis=0, keepdims=True))
        total = total * jnp.exp(high - new) + jnp.sum(jnp.exp(score - new), axis=0, keepdims=True)
        return new, total

    high, total = lax.fori_loop(0, NX, stale, (high, total))

    recv(c_pool)
    every = pool_x[...].reshape(NX * nb, emb)
    items[...] = lax.dot_general(every, weight[...], NN, preferred_element_type=f32).astype(bf16)

    score = lax.dot_general(items[...], all_q, NT, preferred_element_type=f32) * factor
    new = jnp.maximum(high, jnp.max(score, axis=0, keepdims=True))
    total = total * jnp.exp(high - new) + jnp.sum(jnp.exp(score - new), axis=0, keepdims=True)
    for g in range(4):
        part[g, 0:1, :] = new[:, 128 * g : 128 * (g + 1)]
        part[g, 1:2, :] = total[:, 128 * g : 128 * (g + 1)]
    parts[q] = part[q // 4]
    start(c_lse)
    ring_start(3)

    mine = items[pl.ds(pl.multiple_of(x * nb, nb), nb), :]
    own = lax.dot_general(
        mine, q4[...].reshape(4 * nb, dim), NT, preferred_element_type=f32
    ) * factor
    chosen = meta[4:5, :] == lax.broadcasted_iota(i32, (nb, 128), 0)
    hit = jnp.sum(jnp.where(chosen, own, 0.0), axis=0, keepdims=True)
    lanes = lax.broadcasted_iota(i32, (nb, 128), 1) // nb

    ring_start(4)
    recv(c_lse)
    got = parts[...]
    highs, totals = got[:, 0, :], got[:, 1, :]
    top = jnp.max(highs, axis=0, keepdims=True)
    lse = top + jnp.log(jnp.sum(totals * jnp.exp(highs - top), axis=0, keepdims=True))
    lse = jnp.where(lanes[0:1] == q % 4, lse, 0.0)
    lse = lse + pltpu.roll(lse, 64, 1)
    lse = lse + pltpu.roll(lse, 32, 1)
    loss[...] = (lse - hit)[0, 0:nb]
    coef = jnp.exp(own - lse) - jnp.where(chosen, 1.0, 0.0)
    coef_all[z] = jnp.where(lanes == z % 4, coef, 0.0).astype(bf16)
    start(c_coef)
    ring_start(5)

    def gradient(g):
        who = [wrap(z + apart(g, r), NZ) for r in range(4)]
        held = jnp.concatenate([coef_all[w] for w in who], axis=0)
        asked = jnp.concatenate([zq[w] for w in who], axis=0)
        item_grad = (
            lax.dot_general(held, asked, NN, preferred_element_type=f32) * factor
        ).astype(bf16)
        pooled_grad = lax.dot_general(item_grad, weight[...], NT, preferred_element_type=f32) / 16.0
        upper = pooled_grad.astype(bf16)
        parted[0:128, :] = upper
        parted[128:256, :] = (pooled_grad - upper.astype(f32)).astype(bf16)

        def spread(t):
            step = 256
            spot = pl.ds(pl.multiple_of(t * step, step), step)
            added = lax.dot_general(count[g, spot, :], parted[...], NN, preferred_element_type=f32)
            grad[spot, :] = added if g == 0 else grad[spot, :] + added

        loop(0, rows // 256, spread)

    for kind in opened:
        if kind is not c_coef and kind is not c_ring[NZ // 2 - 1]:
            kind.sent()
    recv(c_coef.only(1, 11, 10))
    gradient(0)
    recv(c_coef.only(2, 9, 3, 8))
    gradient(1)
    c_coef.sent()
    c_ring[NZ // 2 - 1].sent()
    recv(c_ring[NZ // 2 - 1], c_coef.only(4, 7, 5, 6))
    gradient(2)


def body(table, item_weight, ids, queries, memory, slot_age, positive):
    nb, dim = queries.shape
    rows, emb = table.shape
    arguments = (table, item_weight, ids.reshape(4, 4 * nb), queries, memory, slot_age, positive)
    vmem = pl.BlockSpec(memory_space=pltpu.VMEM)
    dma = pltpu.SemaphoreType.DMA
    loss, grad = pl.pallas_call(
        kernel,
        out_shape=(
            jax.ShapeDtypeStruct((nb,), f32),
            jax.ShapeDtypeStruct((rows, emb), f32),
        ),
        in_specs=[pl.BlockSpec(memory_space=pltpu.HBM)] * 7,
        out_specs=(vmem, vmem),
        scratch_shapes=[
            pltpu.VMEM((rows, emb), bf16),
            pltpu.VMEM((emb, dim), bf16),
            pltpu.VMEM((8, 128), i32),
            pltpu.VMEM((1, nb), i32),
            pltpu.VMEM((3, nb), i32),
            pltpu.VMEM((8, 128), i32),
            pltpu.VMEM((8, 128), i32),
            pltpu.VMEM((128, 8), i32),
            pltpu.VMEM((NZ, 8, 128), i32),
            pltpu.VMEM((NX, 8, 128), i32),
            pltpu.VMEM((NX, 3, nb, dim), bf16),
            pltpu.VMEM((NC, NY, nb, dim), bf16),
            pltpu.VMEM((NZ, nb, dim), bf16),
            pltpu.VMEM((NZ, nb, emb), f32),
            pltpu.VMEM((NZ, nb, emb), f32),
            pltpu.VMEM((3, nb, emb), f32),
            pltpu.VMEM((NX, nb, emb), bf16),
            pltpu.VMEM((4, 8, 128), f32),
            pltpu.VMEM((NQ, 8, 128), f32),
            pltpu.VMEM((NZ, nb, 128), bf16),
            pltpu.VMEM((3, rows, 256), bf16),
            pltpu.VMEM((4, nb, dim), bf16),
            pltpu.VMEM((NX * nb, dim), bf16),
            pltpu.VMEM((256, emb), bf16),
            dma((12,)),
            dma((NZ,)), dma((NZ,)),
            dma((NX,)), dma((NX,)),
            dma((NX,)), dma((NX,)),
            dma((2,)), dma((2,)),
            dma((NY,)), dma((NY,)),
            dma((NY,)), dma((NY,)),
            dma((2, NZ // 2)), dma((2, NZ // 2)),
            dma((NZ,)), dma((NZ,)),
            dma((3,)), dma((3,)),
            dma((NX,)), dma((NX,)),
            dma((NQ,)), dma((NQ,)),
            dma((NZ,)), dma((NZ,)),
        ],
        compiler_params=pltpu.CompilerParams(
            collective_id=0, has_side_effects=True, vmem_limit_bytes=40 * 1024 * 1024
        ),
        name="step",
    )(*(pltpu.with_memory_space_constraint(a, pltpu.HBM) for a in arguments))
    return loss, grad


def solution(mesh):
    split = P(("wide", "grp"))
    rows = P(("wide", "grp"), None)
    return jax.shard_map(
        body,
        mesh=mesh,
        in_specs=(
            rows, P(), split, rows, P(None, ("wide", "grp"), None), P(None, ("wide", "grp")), rows,
        ),
        out_specs=(split, rows),
        check_vma=False,
    )
```

```python
import math

import jax
import jax.numpy as jnp
from jax import lax
from jax.experimental import pallas as pl
from jax.experimental.pallas import tpu as pltpu
from jax.sharding import PartitionSpec as P

MESH = pl.DeviceIdType.MESH
NX, NY, NC, NZ = 4, 8, 2, 12
NQ = NY * NC
DEAD = -1e30
FAR_Z = (6, 5, 7, 4, 8, 3, 9, 2, 10, 1, 11)
FAR_Q = (4, 12, 3, 5, 11, 13, 2, 6, 10, 14, 1, 7, 9, 15, 8)
FAR_X = (2, 1, 3)
NT = (((1,), (1,)), ((), ()))
NN = (((1,), (0,)), ((), ()))
TN = (((0,), (0,)), ((), ()))
f32, bf16, i32 = jnp.float32, jnp.bfloat16, jnp.int32


def wrap(a, n):
    return jnp.where(a >= n, a - n, a)


class Copies:
    def __init__(self, make, ks):
        self.make, self.ks = make, ks

    def each(self, act):
        if isinstance(self.ks, range):
            lax.fori_loop(self.ks[0], self.ks[-1] + 1, lambda k, t: (act(self.make(k)), t)[1], 0)
        else:
            for k in self.ks:
                act(self.make(k))

    def only(self, *ks):
        return Copies(self.make, ks)

    def start(self):
        self.each(lambda copy: copy.start())

    def recv(self):
        self.each(lambda copy: copy.wait_recv())

    def sent(self):
        self.each(lambda copy: copy.wait_send())


def kernel(
    table_hbm, weight_hbm, ids_hbm, queries_hbm, memory_hbm, ages_hbm, positive_hbm,
    loss, grad,
    table, weight, ids, label, ages, meta, marks, cols,
    meta_z, meta_x, mem_x, yq, zq, psend, precv, relayed, pool_x, part, parts, coef_all,
    count, q4, items, parted,
    ds, ms, mr, xs, xr, es, er, hs, hr, ys, yr, cs, cr, zs, zr, ps, pr, rs, rr, os, orr, ls, lr, gs, gr,
):
    wide = lax.axis_index("wide")
    z = lax.axis_index("grp")
    y, x, c = wide // (NX * NC), (wide // NC) % NX, wide % NC
    q = c * NY + y
    nb, dim = queries_hbm.shape
    factor = 2.0 / math.sqrt(dim)
    rows, emb = table_hbm.shape
    base = (wide * NZ + z) * rows

    def dev(y_, x_, c_, z_):
        return ((y_ * NX + x_) * NC + c_, z_)

    def zdev(k):
        return dev(y, x, c, wrap(z + k, NZ))

    def xdev(k):
        return dev(y, (x + k) % NX, c, z)

    def ydev(k):
        return dev((y + k) % NY, x, c, z)

    def qdev(k):
        qq = (q + k) % NQ
        return dev(qq % NY, x, qq // NY, z)

    def rc(src, dst, s, r, to):
        return pltpu.make_async_remote_copy(src, dst, s, r, device_id=to, device_id_type=MESH)

    def loop(lo, hi, body):
        lax.fori_loop(lo, hi, lambda k, t: (body(k), t)[1], 0)

    opened = []

    def start(*kinds):
        for kind in kinds:
            kind.start()
            opened.append(kind)

    def recv(*kinds):
        for kind in kinds:
            kind.recv()

    loads = [
        pltpu.make_async_copy(src, dst, ds.at[n])
        for n, (src, dst) in enumerate(
            [(ids_hbm, ids.at[0:4]), (positive_hbm, label), (ages_hbm, ages), (memory_hbm, mem_x.at[x])]
            + [(queries_hbm, dst) for dst in [yq.at[c, y], zq.at[z]] + [q4.at[j] for j in range(4)]]
            + [(table_hbm, table), (weight_hbm, weight)]
        )
    ]
    for load in loads:
        load.start()

    barrier = pltpu.get_barrier_semaphore()

    def greet(to):
        pl.semaphore_signal(barrier, inc=1, device_id=to, device_id_type=MESH)

    for k in FAR_Z:
        greet(zdev(k))
    for k in FAR_Q:
        greet(qdev(k))
    for k in FAR_X:
        greet(xdev(k))

    ids[4:8] = jnp.zeros((4, 128), i32)
    marks[...] = jnp.zeros((8, 128), i32)
    for load in loads[:3]:
        load.wait()
    cols[...] = jnp.transpose(ids[...])
    marks[4:5, 0:nb] = label[...]
    marks[5:8, 0:nb] = ages[...]
    spot = lax.broadcasted_iota(i32, (8, 8), 1)
    byte = [cols[pl.ds(b, 8, stride=16), :] for b in range(16)]
    lines = []
    for b in range(4):
        for r in range(4):
            line = jnp.zeros((8, 8), i32)
            for t in range(4):
                line = jnp.where(spot == t, byte[4 * t + b][:, r : r + 1], line)
            lines.append(line)
    lined = jnp.transpose(jnp.concatenate(lines, axis=0))
    marked = marks[...]
    marked = marked + pltpu.roll(marked, 32, 1)
    marked = marked + pltpu.roll(marked, 64, 1)
    own_meta = jnp.where(lax.broadcasted_iota(i32, (8, 128), 0) < 4, lined, marked)
    meta[...] = own_meta
    meta_z[z] = own_meta
    meta_x[x] = own_meta
    for load in loads[3:10]:
        load.wait()
    pl.semaphore_wait(barrier, (NZ - 1) + (NQ - 1) + (NX - 1))

    def ring(s, d):
        owner = wrap(z + s, NZ) if d == 0 else wrap(z - s + NZ, NZ)
        to = zdev(NZ - 1) if d == 0 else zdev(1)
        return rc(zq.at[owner], zq.at[owner], zs.at[d, s], zr.at[d, s], to)

    def half(r):
        block = mem_x.at[(x + 1 + 2 * r) % NX, :, nb // 2 * r : nb // 2 * (r + 1)]
        return rc(block, block, hs.at[r], hr.at[r], xdev(3 - 2 * r))

    def fourth(_):
        block = yq.at[c, (y + 3) % NY]
        return rc(block, block, ys.at[4], yr.at[4], ydev(NY - 1))

    def across(k):
        block = yq.at[c, (y - k + NY) % NY]
        return rc(block, block, cs.at[k], cr.at[k], dev(y, x, 1 - c, z))

    def relay(j):
        to = zdev(jnp.where(j == 2, NZ - 1, 2 - j))
        return rc(psend.at[far(j)], relayed.at[j], rs.at[j], rr.at[j], to)

    def far(j):
        return 6 + (1 - 2 * (j % 2)) * ((j + 1) // 2)

    def apart(g, r):
        u = (r + 1 - z + NZ) % 4
        if g == 0:
            return jnp.where(u == 0, NZ - 1, u - 1)
        return jnp.where(u < 2, u + 3, u + 7) if g == 1 else jnp.where(u < 2, u + 7, u + 3)

    c_meta_z = Copies(lambda k: rc(meta, meta_z.at[z], ms.at[k], mr.at[k], zdev(k)), FAR_Z)
    c_meta_x = Copies(lambda k: rc(meta, meta_x.at[x], xs.at[k], xr.at[k], xdev(k)), range(1, NX))
    c_mem_x = Copies(lambda k: rc(mem_x.at[x], mem_x.at[x], es.at[k], er.at[k], xdev(k)), (1, 3))
    c_half = Copies(half, (0, 1))
    c_q_y = Copies(
        lambda k: rc(yq.at[c, y], yq.at[c, y], ys.at[k], yr.at[k], ydev(k)), (5, 3, 6, 2, 7, 1)
    )
    c_fourth = Copies(fourth, (4,))
    c_across = Copies(across, range(0, NY))
    c_ring = [
        Copies(lambda d, s=s: ring(s, d), (0, 1) if s < NZ // 2 - 1 else (0,)) for s in range(NZ // 2)
    ]
    c_relay = Copies(relay, range(0, 3))
    c_part = Copies(
        lambda k: rc(psend.at[k], precv.at[k], ps.at[k], pr.at[k], zdev(k)), (1, 11, 2, 10, 3, 9, 4, 8)
    )
    c_pool = Copies(
        lambda k: rc(pool_x.at[x], pool_x.at[x], os.at[k], orr.at[k], xdev(k)), FAR_X
    )
    c_lse = Copies(
        lambda k: rc(part.at[((q + k) % NQ) // 4], parts.at[q], ls.at[k], lr.at[k], qdev(k)),
        FAR_Q,
    )
    c_coef = Copies(
        lambda k: rc(coef_all.at[z], coef_all.at[z], gs.at[k], gr.at[k], zdev(k)), FAR_Z
    )

    def ring_start(s):
        if s > 0:
            recv(c_ring[s - 1])
        start(c_ring[s])

    start(c_meta_z, c_q_y.only(5, 3))

    lane = lax.broadcasted_iota(i32, (8, 128), 1) // nb

    def counts(g):
        lined = [jnp.zeros((8, 128), i32) for b in range(4)]
        for r in range(4):
            asked = meta_z[wrap(z + apart(g, r), NZ)] - base
            for b in range(4):
                rolled = asked if r == b else pltpu.roll(asked, ((r - b) * nb) % 128, 1)
                lined[b] = jnp.where(lane == r, rolled, lined[b])
        step = 128

        def block(t):
            spots = lax.broadcasted_iota(i32, (step, 128), 0) + t * step
            found = jnp.zeros((step, 128), f32)
            for b in range(4):
                for r in range(4):
                    found = found + jnp.where(lined[b][r : r + 1, :] == spots, 1.0, 0.0)
            found = found.astype(bf16)
            spot = pl.ds(pl.multiple_of(t * step, step), step)
            count[g, spot, 0:128] = found
            count[g, spot, 128:256] = found

        loop(0, rows // step, block)

    def lookup(g):
        counts(g)
        sums = lax.dot_general(count[g, :, 0:128], table[...], TN, preferred_element_type=f32)
        for r in range(4):
            psend[apart(g, r)] = sums[r * nb : (r + 1) * nb]

    recv(c_meta_z.only(1, 11, 10))
    start(c_meta_x, c_mem_x, c_q_y.only(6, 2, 7, 1), c_across.only(0))
    for load in loads[10:]:
        load.wait()
    lookup(0)
    start(c_part.only(1, 11, 2))
    recv(c_meta_z.only(2, 9, 3, 8))
    ring_start(0)
    lookup(1)
    recv(c_meta_z.only(4, 7, 5, 6))
    lookup(2)
    start(c_relay)
    start(c_part.only(10, 3, 9))
    recv(c_q_y.only(5))
    start(c_fourth)
    recv(c_relay.only(2))
    psend[8] = psend[8] + relayed[2]
    start(c_part.only(8))
    recv(c_relay.only(1, 0))
    psend[4] = psend[4] + (relayed[0] + relayed[1])
    start(c_part.only(4))
    ring_start(1)

    recv(c_mem_x)
    start(c_half)
    for k in (7, 1, 6, 2, 5, 3):
        if k != 5:
            recv(c_q_y.only(k))
        start(c_across.only(k))

    recv(c_part)
    pooled = psend[0]
    for k in (1, 11, 2, 10, 3, 9, 4, 8):
        pooled = pooled + precv[k]
    pool_x[x] = (pooled / 16.0).astype(bf16)
    start(c_pool)
    recv(c_fourth)
    start(c_across.only(4))
    ring_start(2)

    recv(c_meta_x, c_half, c_across)
    all_q = yq[...].reshape(NQ * nb, dim)

    high = jnp.full((1, NQ * nb), DEAD, f32)
    total = jnp.zeros((1, NQ * nb), f32)

    def stale(t, carry):
        high, total = carry
        keys = mem_x[t].reshape(3 * nb, dim)
        score = lax.dot_general(keys, all_q, NT, preferred_element_type=f32) * factor
        marked = jnp.transpose(meta_x[t])
        age = jnp.concatenate([marked[0:nb, 5 + s : 6 + s] for s in range(3)], axis=0)
        score = jnp.where(age <= 3, score, DEAD)
        new = jnp.maximum(high, jnp.max(score, axis=0, keepdims=True))
        total = total * jnp.exp(high - new) + jnp.sum(jnp.exp(score - new), axis=0, keepdims=True)
        return new, total

    high, total = lax.fori_loop(0, NX, stale, (high, total))

    recv(c_pool)
    every = pool_x[...].reshape(NX * nb, emb)
    items[...] = lax.dot_general(every, weight[...], NN, preferred_element_type=f32).astype(bf16)

    score = lax.dot_general(items[...], all_q, NT, preferred_element_type=f32) * factor
    new = jnp.maximum(high, jnp.max(score, axis=0, keepdims=True))
    total = total * jnp.exp(high - new) + jnp.sum(jnp.exp(score - new), axis=0, keepdims=True)
    for g in range(4):
        part[g, 0:1, :] = new[:, 128 * g : 128 * (g + 1)]
        part[g, 1:2, :] = total[:, 128 * g : 128 * (g + 1)]
    parts[q] = part[q // 4]
    start(c_lse)
    ring_start(3)

    mine = items[pl.ds(pl.multiple_of(x * nb, nb), nb), :]
    own = lax.dot_general(
        mine, q4[...].reshape(4 * nb, dim), NT, preferred_element_type=f32
    ) * factor
    chosen = meta[4:5, :] == lax.broadcasted_iota(i32, (nb, 128), 0)
    hit = jnp.sum(jnp.where(chosen, own, 0.0), axis=0, keepdims=True)
    lanes = lax.broadcasted_iota(i32, (nb, 128), 1) // nb

    ring_start(4)
    recv(c_lse)
    got = parts[...]
    highs, totals = got[:, 0, :], got[:, 1, :]
    top = jnp.max(highs, axis=0, keepdims=True)
    lse = top + jnp.log(jnp.sum(totals * jnp.exp(highs - top), axis=0, keepdims=True))
    lse = jnp.where(lanes[0:1] == q % 4, lse, 0.0)
    lse = lse + pltpu.roll(lse, 64, 1)
    lse = lse + pltpu.roll(lse, 32, 1)
    loss[...] = (lse - hit)[0, 0:nb]
    coef = jnp.exp(own - lse) - jnp.where(chosen, 1.0, 0.0)
    coef_all[z] = jnp.where(lanes == z % 4, coef, 0.0).astype(bf16)
    start(c_coef)
    ring_start(5)

    def gradient(g):
        who = [wrap(z + apart(g, r), NZ) for r in range(4)]
        held = jnp.concatenate([coef_all[w] for w in who], axis=0)
        asked = jnp.concatenate([zq[w] for w in who], axis=0)
        item_grad = (
            lax.dot_general(held, asked, NN, preferred_element_type=f32) * factor
        ).astype(bf16)
        pooled_grad = lax.dot_general(item_grad, weight[...], NT, preferred_element_type=f32) / 16.0
        upper = pooled_grad.astype(bf16)
        parted[0:128, :] = upper
        parted[128:256, :] = (pooled_grad - upper.astype(f32)).astype(bf16)

        def spread(t):
            step = 512
            spot = pl.ds(pl.multiple_of(t * step, step), step)
            added = lax.dot_general(count[g, spot, :], parted[...], NN, preferred_element_type=f32)
            grad[spot, :] = added if g == 0 else grad[spot, :] + added

        loop(0, rows // 512, spread)

    for kind in opened:
        if kind is not c_coef and kind is not c_ring[NZ // 2 - 1]:
            kind.sent()
    recv(c_coef.only(1, 11, 10))
    gradient(0)
    recv(c_coef.only(2, 9, 3, 8))
    gradient(1)
    c_coef.sent()
    c_ring[NZ // 2 - 1].sent()
    recv(c_ring[NZ // 2 - 1], c_coef.only(4, 7, 5, 6))
    gradient(2)


def body(table, item_weight, ids, queries, memory, slot_age, positive):
    nb, dim = queries.shape
    rows, emb = table.shape
    arguments = (table, item_weight, ids.reshape(4, 4 * nb), queries, memory, slot_age, positive)
    vmem = pl.BlockSpec(memory_space=pltpu.VMEM)
    dma = pltpu.SemaphoreType.DMA
    loss, grad = pl.pallas_call(
        kernel,
        out_shape=(
            jax.ShapeDtypeStruct((nb,), f32),
            jax.ShapeDtypeStruct((rows, emb), f32),
        ),
        in_specs=[pl.BlockSpec(memory_space=pltpu.HBM)] * 7,
        out_specs=(vmem, vmem),
        scratch_shapes=[
            pltpu.VMEM((rows, emb), bf16),
            pltpu.VMEM((emb, dim), bf16),
            pltpu.VMEM((8, 128), i32),
            pltpu.VMEM((1, nb), i32),
            pltpu.VMEM((3, nb), i32),
            pltpu.VMEM((8, 128), i32),
            pltpu.VMEM((8, 128), i32),
            pltpu.VMEM((128, 8), i32),
            pltpu.VMEM((NZ, 8, 128), i32),
            pltpu.VMEM((NX, 8, 128), i32),
            pltpu.VMEM((NX, 3, nb, dim), bf16),
            pltpu.VMEM((NC, NY, nb, dim), bf16),
            pltpu.VMEM((NZ, nb, dim), bf16),
            pltpu.VMEM((NZ, nb, emb), f32),
            pltpu.VMEM((NZ, nb, emb), f32),
            pltpu.VMEM((3, nb, emb), f32),
            pltpu.VMEM((NX, nb, emb), bf16),
            pltpu.VMEM((4, 8, 128), f32),
            pltpu.VMEM((NQ, 8, 128), f32),
            pltpu.VMEM((NZ, nb, 128), bf16),
            pltpu.VMEM((3, rows, 256), bf16),
            pltpu.VMEM((4, nb, dim), bf16),
            pltpu.VMEM((NX * nb, dim), bf16),
            pltpu.VMEM((256, emb), bf16),
            dma((12,)),
            dma((NZ,)), dma((NZ,)),
            dma((NX,)), dma((NX,)),
            dma((NX,)), dma((NX,)),
            dma((2,)), dma((2,)),
            dma((NY,)), dma((NY,)),
            dma((NY,)), dma((NY,)),
            dma((2, NZ // 2)), dma((2, NZ // 2)),
            dma((NZ,)), dma((NZ,)),
            dma((3,)), dma((3,)),
            dma((NX,)), dma((NX,)),
            dma((NQ,)), dma((NQ,)),
            dma((NZ,)), dma((NZ,)),
        ],
        compiler_params=pltpu.CompilerParams(
            collective_id=0, has_side_effects=True, vmem_limit_bytes=40 * 1024 * 1024
        ),
        name="step",
    )(*(pltpu.with_memory_space_constraint(a, pltpu.HBM) for a in arguments))
    return loss, grad


def solution(mesh):
    split = P(("wide", "grp"))
    rows = P(("wide", "grp"), None)
    return jax.shard_map(
        body,
        mesh=mesh,
        in_specs=(
            rows, P(), split, rows, P(None, ("wide", "grp"), None), P(None, ("wide", "grp")), rows,
        ),
        out_specs=(split, rows),
        check_vma=False,
    )
```
